256 devices in a mesh: dp: 2 (over y_lo), stretch: 16 (over x, y_hi, core), head: 8 (over z).
Axes of the slice: x: 4, y: 4 (y_hi: 2, y_lo: 2; y = y_hi * 2 + y_lo), z: 8, core: 2. Of those that a mesh axis runs over, the one named last changes fastest.
Arguments:
- queries: bfloat16 [32768, 2048], P(('dp', 'stretch', 'head')), parts along dimension 0, may hold values from -6 to 6
- key_heads: bfloat16 [32768, 256], P(('dp', 'stretch', 'head')), parts along dimension 0, may hold values from -6 to 6
- value_heads: bfloat16 [32768, 256], P(('dp', 'stretch', 'head')), parts along dimension 0, may hold values from -6 to 6
- out_grad: bfloat16 [32768, 2048], P(('dp', 'stretch', 'head')), parts along dimension 0, may hold values from -6 to 6
- lengths: int32 [128], P('dp'), parts along dimension 0, may hold values from 1 to 2048, 16384 in all
Outputs:
- attended: bfloat16 [32768, 2048], P(('dp', 'stretch', 'head')), parts along dimension 0
- query_grad: bfloat16 [32768, 2048], P(('dp', 'stretch', 'head')), parts along dimension 0
- key_grad: bfloat16 [32768, 256], P(('dp', 'stretch', 'head')), parts along dimension 0
- value_grad: bfloat16 [32768, 256], P(('dp', 'stretch', 'head')), parts along dimension 0
The draws below stay inside these ranges and needn't reach their ends.
There are 2 independent parts, one for each index of `dp`. The reference program is written for one: setup_inputs(seed, part) draws one part's arguments, and reference() takes and returns one part's arrays. A program takes and returns all parts, laid end to end along the dimension named above; each array names one. Nothing has to cross between parts.
Inputs may be any that keep to these rules, and one draw needn't show every extreme that they name: The lengths sum to 16384.
All inputs are finite; a program needn't handle non-finite values.
Results may differ from the reference program's by a relative error of at most 0.029.
Values may be sent and summed in bfloat16 or wider, within the bound.
No kernel may reach another device: no remote copies, remote signals or barrier semaphores. Data moves between devices by JAX's collectives and lax.ppermute only.
A program may use at most 128 MiB of HBM per device.

```python
import math
import jax
import jax.numpy as jnp
import numpy as np
from jax import lax

HD = 128
QH = 16
KVH = 2
SPAN_CH = 2
STRETCH = 1024
STREAM = 16384
MAXLEN = 2048
NDOC = 64


def draw_queries(key, part):
    key = jax.random.fold_in(key, 11)
    drawn = jax.random.truncated_normal(key, -6.0, 6.0, (STREAM, QH * HD))
    return drawn.astype(jnp.bfloat16)


def draw_key_heads(key, part):
    key = jax.random.fold_in(key, 23)
    drawn = jax.random.truncated_normal(key, -6.0, 6.0, (STREAM, KVH * HD))
    return drawn.astype(jnp.bfloat16)


def block_levels(key, dims, pieces, smallest, largest):
    level = 1.0
    for axis_at, parts in pieces:
        draws = jax.random.uniform(jax.random.fold_in(jax.random.fold_in(key, 6), axis_at), (parts,), jnp.float32, smallest / len(pieces), largest / len(pieces))
        level = level * jnp.repeat(jnp.exp(draws), dims[axis_at] // parts).reshape((-1,) + (1,) * (len(dims) - 1 - axis_at))
    return level


def length_profile(number_of, total, limit, skew):
    weights = [(1 << 20) // math.isqrt(rank ** skew) + 1 for rank in range(2, number_of + 1)]
    spare, given = total - limit - (number_of - 1), [1] * (number_of - 1)
    while spare > 0:
        free = [i for i in range(number_of - 1) if given[i] < limit]
        pool, budget = sum([weights[i] for i in free]), spare
        for i in free:
            addition = min(limit - given[i], max(1, budget * weights[i] // pool), spare)
            given[i] = given[i] + addition
            spare = spare - addition
    return np.array([limit] + given)


def ragged(stream_key, amount, total, bound, slope):
    if amount == 2:
        one = jax.random.randint(stream_key, (), max(1, total - bound), min(bound, total - 1) + 1)
        return jnp.stack([one, total - one])
    sizes = jnp.asarray(length_profile(amount, total, bound, slope), jnp.int32)
    couples = (amount - 1) // 2
    source_of, sink = sizes[1:1 + 2 * couples:2], sizes[2:2 + 2 * couples:2]
    room = jnp.minimum(source_of - 1, bound - sink)
    passed = jax.random.randint(jax.random.fold_in(stream_key, 1), (couples,), 0, 1 << 20) % (room + 1)
    sizes = sizes.at[1:1 + 2 * couples:2].set(source_of - passed).at[2:2 + 2 * couples:2].set(sink + passed)
    return sizes[jax.random.permutation(jax.random.fold_in(stream_key, 2), amount)]


def noise(key, shape, scale, bound, cuts=(), kind=jnp.bfloat16):
    loudness = block_levels(key, shape, cuts, -0.22, 0.18) if cuts else 1.0
    entries = jax.random.normal(key, shape, jnp.float32) * scale * loudness
    return jnp.minimum(jnp.maximum(entries, -bound), bound).astype(kind)


def setup_inputs(seed: int = 0, part: int = 0) -> dict:
    streams_of = jax.random.split(jax.random.key(seed), 6)
    own_keys = jax.random.split(jax.random.fold_in(streams_of[5], part), 6)
    return {
        "queries": draw_queries(jax.random.fold_in(jax.random.fold_in(streams_of[5], part), 71), part),
        "key_heads": draw_key_heads(jax.random.fold_in(jax.random.fold_in(streams_of[5], part), 71), part),
        "value_heads": noise(own_keys[2], (STREAM, KVH * HD), 1.0, 6.0, ((0, 128),)),
        "out_grad": noise(own_keys[3], (STREAM, QH * HD), 1.0, 6.0, ((0, 128),)),
        "lengths": ragged(own_keys[4], NDOC, STREAM, MAXLEN, 2).astype(jnp.int32),
    }


def document_of(lengths, positions):
    starts = jnp.cumsum(lengths) - lengths
    return jnp.sum((starts[None, :] <= positions[:, None]).astype(jnp.int32), axis=1) - 1


def reference(queries, key_heads, value_heads, out_grad, lengths):
    score_scale = HD ** -0.5
    group_size = QH // KVH
    reach = SPAN_CH * STRETCH
    window = reach + STRETCH
    block_count = STREAM // STRETCH
    front = jnp.zeros((reach, KVH * HD), jnp.bfloat16)
    keys_padded = jnp.concatenate([front, key_heads], axis=0)
    values_padded = jnp.concatenate([front, value_heads], axis=0)

    def one_block(carry, block_index):
        key_total, value_total = carry
        start = (block_index * STRETCH).astype(jnp.int32)
        query_block = lax.dynamic_slice_in_dim(queries, start, STRETCH, 0).astype(jnp.float32).reshape(STRETCH, KVH, group_size, HD)
        grad_block = lax.dynamic_slice_in_dim(out_grad, start, STRETCH, 0).astype(jnp.float32).reshape(STRETCH, KVH, group_size, HD)
        key_window = lax.dynamic_slice_in_dim(keys_padded, start, window, 0).astype(jnp.float32).reshape(window, KVH, HD)
        value_window = lax.dynamic_slice_in_dim(values_padded, start, window, 0).astype(jnp.float32).reshape(window, KVH, HD)
        query_pos = start + jnp.arange(STRETCH, dtype=jnp.int32)
        key_pos = start - reach + jnp.arange(window, dtype=jnp.int32)
        allowed = (document_of(lengths, query_pos)[:, None] == document_of(lengths, key_pos)[None, :]) & (key_pos[None, :] <= query_pos[:, None])
        scores = jnp.einsum("qgjd,kgd->gjqk", query_block, key_window) * score_scale
        scores = jnp.where(allowed[None, None], scores, -jnp.inf)
        row_top = jnp.max(scores, axis=-1, keepdims=True)
        expanded = jnp.exp(scores - row_top)
        softmax = expanded / jnp.sum(expanded, axis=-1, keepdims=True)
        rounded_softmax = lax.optimization_barrier(softmax.astype(jnp.bfloat16)).astype(jnp.float32)
        attended = jnp.einsum("gjqk,kgd->qgjd", rounded_softmax, value_window).astype(jnp.bfloat16)
        attended_wide = lax.optimization_barrier(attended).astype(jnp.float32)
        correction = jnp.einsum("qgjd,qgjd->gjq", grad_block, attended_wide)
        softmax_grad = jnp.einsum("qgjd,kgd->gjqk", grad_block, value_window)
        score_grad = softmax * (softmax_grad - correction[..., None])
        rounded_grad = lax.optimization_barrier(score_grad.astype(jnp.bfloat16)).astype(jnp.float32)
        query_grad = (jnp.einsum("gjqk,kgd->qgjd", rounded_grad, key_window) * score_scale).astype(jnp.bfloat16)
        key_part = jnp.einsum("gjqk,qgjd->kgd", rounded_grad, query_block) * score_scale
        value_part = jnp.einsum("gjqk,qgjd->kgd", rounded_softmax, grad_block)
        key_total = lax.dynamic_update_slice_in_dim(key_total, lax.dynamic_slice_in_dim(key_total, start, window, 0) + key_part.reshape(window, KVH * HD), start, 0)
        value_total = lax.dynamic_update_slice_in_dim(value_total, lax.dynamic_slice_in_dim(value_total, start, window, 0) + value_part.reshape(window, KVH * HD), start, 0)
        return (key_total, value_total), (attended.reshape(STRETCH, QH * HD), query_grad.reshape(STRETCH, QH * HD))

    initial = (jnp.zeros((reach + STREAM, KVH * HD), jnp.float32), jnp.zeros((reach + STREAM, KVH * HD), jnp.float32))
    (key_total, value_total), (attended_blocks, query_blocks) = lax.scan(one_block, initial, jnp.arange(block_count, dtype=jnp.int32))
    attended = attended_blocks.reshape(STREAM, QH * HD)
    query_grad = query_blocks.reshape(STREAM, QH * HD)
    key_grad = key_total[reach:].astype(jnp.bfloat16)
    value_grad = value_total[reach:].astype(jnp.bfloat16)
    return (attended, query_grad, key_grad, value_grad)
```

```python
import jax
import jax.numpy as jnp
from jax import lax
from jax.experimental import pallas as pl
from jax.experimental.pallas import tpu as pltpu
from jax.sharding import PartitionSpec as P

HD = 128
GROUP = 8
ROWS = 128
WIDE = GROUP * HD
LANES = GROUP * ROWS
RING = 8
KB = 256
SPAN = 2048
SCALE = HD**-0.5
EXP2 = SCALE * 1.4426950408889634
LOW = -1e30


def dot(x, y, cx, cy):
    return lax.dot_general(
        x, y, (((cx,), (cy,)), ((), ())), preferred_element_type=jnp.float32
    )


def attend_kernel(info, dst, qo, qx, go, gx, *refs):
    kv_refs = refs[:9]
    att_refs = refs[9:11]
    dq_refs = refs[11:13]
    part_refs = refs[13:21]
    q_s, g_s, k_s, v_s, dk_s, dv_s, s_s, o_s = refs[21:]
    h, core = info[0], info[1]
    base = pl.multiple_of(core * WIDE, WIDE)
    for n in range(GROUP):
        rows = slice(n * ROWS, (n + 1) * ROWS)
        cols = slice(n * HD, (n + 1) * HD)
        q_s[0, rows, :] = qo[:, pl.ds(base + n * HD, HD)]
        g_s[0, rows, :] = go[:, pl.ds(base + n * HD, HD)]
        q_s[1, rows, :] = qx[:, cols]
        g_s[1, rows, :] = gx[:, cols]

    def row_of(rel, piece):
        j = lax.rem(h + (rel + RING), RING)
        side = core if piece % 2 == 0 else 1 - core
        chunk = j + 8 * side + (16 if piece < 2 else 0)
        return pl.multiple_of(chunk * ROWS, ROWS)

    held = [(rel, p, kv_refs[i], p) for i, rel in enumerate((0, -1, -2, -3, 1, 2, 3)) for p in range(4)]
    held += [(4, p, kv_refs[7], p) for p in (0, 1)] + [(4, p, kv_refs[8], p - 2) for p in (2, 3)]
    for rel, piece, ref, at in held:
        row = row_of(rel, piece)
        k_s[pl.ds(row, ROWS), :] = ref[at * ROWS : (at + 1) * ROWS, :HD]
        v_s[pl.ds(row, ROWS), :] = ref[at * ROWS : (at + 1) * ROWS, HD:]
    dk_s[...] = jnp.zeros_like(dk_s)
    dv_s[...] = jnp.zeros_like(dv_s)

    for slot in range(2):
        side = core if slot == 0 else 1 - core
        first = SPAN + (h + 8 * side) * ROWS
        low = info[2 + slot] // KB
        high = (first + ROWS - 1) // KB + 1
        start = jnp.concatenate([dst[slot : slot + 1, :]] * GROUP, axis=1)
        place = jnp.concatenate(
            [first + lax.broadcasted_iota(jnp.int32, (1, ROWS), 1)] * GROUP, axis=1
        )

        def scores(b, top):
            key_row = pl.multiple_of(b * KB, KB)
            raw = dot(k_s[pl.ds(key_row, KB), :], q_s[slot], 1, 1)
            key_place = key_row + lax.broadcasted_iota(jnp.int32, (KB, LANES), 0)
            raw = jnp.where((key_place >= start) & (key_place <= place), raw, LOW)
            s_s[pl.ds(pl.multiple_of((b - low) * KB, KB), KB), :] = raw
            return jnp.maximum(top, jnp.max(raw.reshape(KB // 8, 8, LANES), axis=0))

        top = lax.fori_loop(low, high, scores, jnp.full((8, LANES), LOW, jnp.float32))
        top = jnp.max(top, axis=0, keepdims=True)
        o_s[...] = jnp.zeros_like(o_s)

        def forward(b, total):
            key_row = pl.multiple_of(b * KB, KB)
            at = pl.ds(pl.multiple_of((b - low) * KB, KB), KB)
            weight = jnp.exp2((s_s[at, :] - top) * EXP2)
            s_s[at, :] = weight
            o_s[...] += dot(v_s[pl.ds(key_row, KB), :], weight.astype(jnp.bfloat16), 0, 0)
            return total + jnp.sum(weight.reshape(KB // 8, 8, LANES), axis=0)

        total = lax.fori_loop(low, high, forward, jnp.zeros((8, LANES), jnp.float32))
        inverse = 1.0 / jnp.sum(total, axis=0, keepdims=True)
        corrections = []
        for n in range(GROUP):
            cols = slice(n * HD, (n + 1) * HD)
            rows = slice(n * ROWS, (n + 1) * ROWS)
            att = jnp.transpose(o_s[:, rows] * inverse[:, rows]).astype(jnp.bfloat16)
            att_refs[slot][:, cols] = att
            product = att.astype(jnp.float32) * g_s[slot, rows, :].astype(jnp.float32)
            corrections.append(jnp.sum(jnp.transpose(product), axis=0, keepdims=True))
        correction = jnp.concatenate(corrections, axis=1)
        o_s[...] = jnp.zeros_like(o_s)

        def backward(b, carry):
            key_row = pl.multiple_of(b * KB, KB)
            at = pl.ds(pl.multiple_of((b - low) * KB, KB), KB)
            keys = pl.ds(key_row, KB)
            weight = s_s[at, :] * inverse
            weight_grad = dot(v_s[keys, :], g_s[slot], 1, 1)
            score_grad = (weight * (weight_grad - correction)).astype(jnp.bfloat16)
            dv_s[keys, :] += dot(weight.astype(jnp.bfloat16), g_s[slot], 1, 0)
            dk_s[keys, :] += dot(score_grad, q_s[slot], 1, 0)
            o_s[...] += dot(k_s[keys, :], score_grad, 0, 0)
            return carry

        lax.fori_loop(low, high, backward, 0)
        for n in range(GROUP):
            cols = slice(n * HD, (n + 1) * HD)
            rows = slice(n * ROWS, (n + 1) * ROWS)
            dq_refs[slot][:, cols] = jnp.transpose(o_s[:, rows] * SCALE).astype(jnp.bfloat16)

    for i, rel in enumerate((0, 1, 2, 3, 4, -1, -2, -3)):
        for piece in range(4):
            at = slice(piece * ROWS, (piece + 1) * ROWS)
            row = row_of(rel, piece)
            kind = part_refs[i].dtype
            part_refs[i][at, :HD] = (dk_s[pl.ds(row, ROWS), :] * SCALE).astype(kind)
            part_refs[i][at, HD:] = dv_s[pl.ds(row, ROWS), :].astype(kind)


def attend(info, starts, operands):
    bf16 = jnp.bfloat16
    side = jax.ShapeDtypeStruct((ROWS, WIDE), bf16)
    parts = [jax.ShapeDtypeStruct((4 * ROWS, 2 * HD), jnp.float32 if i == 0 else bf16) for i in range(8)]
    whole = pl.BlockSpec(memory_space=pltpu.VMEM)
    return pl.pallas_call(
        attend_kernel,
        in_specs=[pl.BlockSpec(memory_space=pltpu.SMEM)] + [whole] * (1 + len(operands)),
        out_specs=[whole] * 12,
        out_shape=[side] * 4 + parts,
        scratch_shapes=[
            pltpu.VMEM((2, LANES, HD), bf16),
            pltpu.VMEM((2, LANES, HD), bf16),
            pltpu.VMEM((2 * SPAN, HD), bf16),
            pltpu.VMEM((2 * SPAN, HD), bf16),
            pltpu.VMEM((2 * SPAN, HD), jnp.float32),
            pltpu.VMEM((2 * SPAN, HD), jnp.float32),
            pltpu.VMEM((SPAN + KB, LANES), jnp.float32),
            pltpu.VMEM((HD, LANES), jnp.float32),
        ],
        compiler_params=pltpu.CompilerParams(vmem_limit_bytes=48 * 1024 * 1024),
        name="attend",
    )(info, starts, *operands)


def add(*terms):
    return sum(term.astype(jnp.float32) for term in terms).astype(jnp.bfloat16)


def body(queries, key_heads, value_heads, out_grad, lengths):
    count = lax.axis_size("stretch")
    stretch = lax.axis_index("stretch")
    h = lax.axis_index("head")
    core = lax.rem(stretch, 2)
    swap = [(s, s ^ 1) for s in range(count)]
    same = [(s, s + 2) for s in range(count - 2)]
    cross = [(s, (s ^ 1) + 2) for s in range(count - 2)]
    up = [(i, (i + 1) % RING) for i in range(RING)]
    down = [(i, (i - 1) % RING) for i in range(RING)]

    def back(pairs):
        return [(target, source) for source, target in pairs]

    def half(array, which, width):
        return lax.dynamic_slice_in_dim(array, which * width, width, axis=1)

    def pair(which):
        return jnp.concatenate([half(key_heads, which, HD), half(value_heads, which, HD)], axis=1)

    mine, other = pair(core), pair(1 - core)
    held = jnp.concatenate(
        [
            mine,
            lax.ppermute(other, "stretch", swap),
            lax.ppermute(mine, "stretch", same),
            lax.ppermute(other, "stretch", cross),
        ],
        axis=0,
    )
    query_other = lax.ppermute(half(queries, 1 - core, WIDE), "stretch", swap)
    grad_other = lax.ppermute(half(out_grad, 1 - core, WIDE), "stretch", swap)

    ups, downs = [held], [held]
    for _ in range(3):
        ups.append(lax.ppermute(ups[-1], "head", up))
        downs.append(lax.ppermute(downs[-1], "head", down))
    middle = 2 * ROWS
    far_own = lax.ppermute(ups[-1][:middle], "head", up)
    far_past = lax.ppermute(downs[-1][middle:], "head", down)

    line = stretch // 2
    origin = (line - 1) * SPAN
    order = jnp.arange(lengths.shape[0], dtype=jnp.int32)
    starts = jnp.sum(jnp.where(order[:, None] < order[None, :], lengths[:, None], 0), axis=0)
    chunk = jnp.stack([h + 8 * core, h + 8 * (1 - core)])
    places = line * SPAN + chunk[:, None] * ROWS + jnp.arange(ROWS, dtype=jnp.int32)[None, :]
    first = jnp.max(jnp.where(starts <= places[..., None], starts, 0), axis=-1) - origin
    info = jnp.stack([h, core, first[0, 0], first[1, 0]]).astype(jnp.int32)

    outs = attend(
        info,
        first,
        [queries, query_other, out_grad, grad_other, held, *ups[1:], *downs[1:], far_own, far_past],
    )
    att_own, att_other, dq_own, dq_other, here = outs[:5]
    above, below = outs[5:9], outs[9:12]

    def assemble(own, swapped):
        return jnp.where(
            core == 0,
            jnp.concatenate([own, swapped], axis=1),
            jnp.concatenate([swapped, own], axis=1),
        )

    rising = lax.ppermute(above[3][:middle], "head", up)
    falling = lax.ppermute(above[3][middle:], "head", down)
    rising = jnp.concatenate([add(rising, above[2][:middle]), above[2][middle:]], axis=0)
    falling = jnp.concatenate([below[2][:middle], add(falling, below[2][middle:])], axis=0)
    for step in (1, 0):
        rising = add(lax.ppermute(rising, "head", up), above[step])
        falling = add(lax.ppermute(falling, "head", down), below[step])
    rising = lax.ppermute(rising, "head", up)
    falling = lax.ppermute(falling, "head", down)

    attended = assemble(att_own, lax.ppermute(att_other, "stretch", swap))
    query_grad = assemble(dq_own, lax.ppermute(dq_other, "stretch", swap))

    def piece(n):
        at = slice(n * ROWS, (n + 1) * ROWS)
        return here[at] + rising[at].astype(jnp.float32) + falling[at].astype(jnp.float32)

    past_same = lax.ppermute(piece(2).astype(jnp.bfloat16), "stretch", back(same))
    past_cross = lax.ppermute(piece(3).astype(jnp.bfloat16), "stretch", back(cross))
    own_other = lax.ppermute(piece(1).astype(jnp.bfloat16), "stretch", swap)
    own = add(piece(0), past_same)
    others = add(own_other, past_cross)
    key_grad = assemble(own[:, :HD], others[:, :HD])
    value_grad = assemble(own[:, HD:], others[:, HD:])
    return attended, query_grad, key_grad, value_grad


def solution(mesh):
    spec = P(("dp", "stretch", "head"), None)
    return jax.shard_map(
        body,
        mesh=mesh,
        in_specs=(spec, spec, spec, spec, P("dp")),
        out_specs=(spec,) * 4,
        check_vma=False,
    )
```

```python
import jax
import jax.numpy as jnp
from jax import lax
from jax.experimental import pallas as pl
from jax.experimental.pallas import tpu as pltpu
from jax.sharding import PartitionSpec as P

HD = 128
GROUP = 8
ROWS = 128
WIDE = GROUP * HD
LANES = GROUP * ROWS
RING = 8
DISTANCES = ((0, 1), (-1, -2), (2, 3), (-3, -4))
REACH = 17 * ROWS
TILE = 4 * ROWS
SPAN = 2048
SCALE = HD**-0.5
EXP2 = SCALE * 1.4426950408889634
LOW = -1e30


def dot(x, y, cx, cy):
    return lax.dot_general(
        x, y, (((cx,), (cy,)), ((), ())), preferred_element_type=jnp.float32
    )


def attend_kernel(info, lengths, qo, go, come, *refs):
    kv_refs = refs[:8]
    att_own, dq_own, other = refs[8:11]
    part_refs = refs[11:21]
    q_s, g_s, k_s, v_s, dk_s, dv_s, s_s, w_s, o_s, top_s, sum_s, high_s, low_s, p_s, h_s, sems = refs[21:]
    outputs = ((att_own, dq_own, 0), (other, other, WIDE))
    h, core = info[0], lax.rem(info[1], 2)
    origin = (info[1] // 2 - 1) * SPAN
    base = pl.multiple_of(core * WIDE, WIDE)
    for n in range(GROUP):
        rows = slice(n * ROWS, (n + 1) * ROWS)
        q_s[0, rows, :] = qo[:, pl.ds(base + n * HD, HD)]
        g_s[0, rows, :] = go[:, pl.ds(base + n * HD, HD)]
        q_s[1, rows, :] = come[:, n * HD : (n + 1) * HD]
        g_s[1, rows, :] = come[:, WIDE + n * HD : WIDE + (n + 1) * HD]
    sign = 1 - 2 * lax.rem(h + core, 2)

    def row_of(distance, past, piece):
        j = lax.rem(h + sign * distance + RING, RING)
        side = core if piece == 0 else 1 - core
        chunk = j + 8 * side + (0 if past else 16)
        return pl.multiple_of(chunk * ROWS, ROWS)

    places = [
        (4 * past + i, 2 * at + piece, row_of(distance, past, piece))
        for past in range(2)
        for i, pair in enumerate(DISTANCES)
        for at, distance in enumerate(pair)
        for piece in range(2)
    ]
    for array, at, row in places:
        k_s[pl.ds(row, ROWS), :] = kv_refs[array][at * ROWS : (at + 1) * ROWS, :HD]
        v_s[pl.ds(row, ROWS), :] = kv_refs[array][at * ROWS : (at + 1) * ROWS, HD:]
    dk_s[...] = jnp.zeros_like(dk_s)
    dv_s[...] = jnp.zeros_like(dv_s)

    for slot in range(2):
        side = core if slot == 0 else 1 - core
        first = SPAN + (h + 8 * side) * ROWS
        place = first + lax.broadcasted_iota(jnp.int32, (1, ROWS), 1)

        begin = reach = -origin
        start = jnp.full((1, ROWS), begin, jnp.int32)
        for i in range(lengths.shape[0] - 1):
            begin += lengths[i]
            reach = jnp.where(begin <= first, begin, reach)
            start = jnp.where(begin <= place, begin, start)
        low = reach // ROWS * ROWS
        chunks = (first + ROWS - low) // ROWS
        tiles = chunks // 4

        def over_keys(visit):
            def tile(b, carry):
                visit(pl.multiple_of(b * TILE, TILE), TILE)
                return carry

            lax.fori_loop(0, tiles, tile, 0)

            @pl.when(chunks % 4 >= 2)
            def _():
                visit(pl.multiple_of(tiles * TILE, TILE), 2 * ROWS)

            @pl.when(chunks % 2 == 1)
            def _():
                visit(pl.multiple_of((chunks - 1) * ROWS, ROWS), ROWS)

        start = jnp.concatenate([start] * GROUP, axis=1)
        place = jnp.concatenate([place] * GROUP, axis=1)

        def scores(at, size):
            row = pl.multiple_of(low + at, ROWS)
            raw = dot(k_s[pl.ds(row, size), :], q_s[slot], 1, 1)
            key_place = row + lax.broadcasted_iota(jnp.int32, (size, LANES), 0)
            raw = jnp.where((key_place >= start) & (key_place <= place), raw, LOW)
            s_s[pl.ds(at, size), :] = raw
            top_s[...] = jnp.maximum(top_s[...], jnp.max(raw.reshape(size // 8, 8, LANES), axis=0))

        top_s[...] = jnp.full_like(top_s, LOW)
        over_keys(scores)
        top = jnp.max(top_s[...], axis=0, keepdims=True)
        sum_s[...] = jnp.zeros_like(sum_s)
        o_s[...] = jnp.zeros_like(o_s)

        def forward(at, size):
            row = pl.multiple_of(low + at, ROWS)
            weight = jnp.exp2((s_s[pl.ds(at, size), :] - top) * EXP2)
            rounded = weight.astype(jnp.bfloat16)
            w_s[pl.ds(at, size), :] = rounded
            o_s[...] += dot(v_s[pl.ds(row, size), :], rounded, 0, 0)
            sum_s[...] += jnp.sum(weight.reshape(size // 8, 8, LANES), axis=0)

        over_keys(forward)
        inverse = 1.0 / jnp.sum(sum_s[...], axis=0, keepdims=True)
        wide = jnp.broadcast_to(inverse, (8, LANES))
        for n in range(GROUP):
            cols = slice(n * HD, (n + 1) * HD)
            rows = slice(n * ROWS, (n + 1) * ROWS)
            att = jnp.transpose((o_s[:, rows] * inverse[:, rows]).astype(jnp.bfloat16))
            outputs[slot][0][:, cols] = att
            column = jnp.transpose(wide[:, rows])[:, :1]
            scaled = (g_s[slot, rows, :].astype(jnp.float32) * column).astype(jnp.bfloat16)
            g_s[slot, rows, :] = scaled
            product = att.astype(jnp.float32) * scaled.astype(jnp.float32)
            high_s[rows, :] = product.astype(jnp.bfloat16)
            low_s[rows, :] = (product - product.astype(jnp.bfloat16).astype(jnp.float32)).astype(jnp.bfloat16)
        ones = jnp.ones((8, HD), jnp.bfloat16)
        correction = (dot(ones, high_s[...], 1, 1) + dot(ones, low_s[...], 1, 1))[:1]
        o_s[...] = jnp.zeros_like(o_s)

        def backward(at, size):
            keys = pl.ds(pl.multiple_of(low + at, ROWS), size)
            weight = w_s[pl.ds(at, size), :]
            weight_grad = dot(v_s[keys, :], g_s[slot], 1, 1)
            score_grad = weight.astype(jnp.float32) * (weight_grad - correction)
            score_grad = score_grad.astype(jnp.bfloat16)
            dv_s[keys, :] += dot(weight, g_s[slot], 1, 0)
            dk_s[keys, :] += dot(score_grad, q_s[slot], 1, 0)
            o_s[...] += dot(k_s[keys, :], score_grad, 0, 0)

        over_keys(backward)
        for n in range(GROUP):
            _, into, offset = outputs[slot]
            rows = slice(n * ROWS, (n + 1) * ROWS)
            query_grad = jnp.transpose((o_s[:, rows] * SCALE).astype(jnp.bfloat16))
            into[:, offset + n * HD : offset + (n + 1) * HD] = query_grad

    copies = []
    for array, at, row in places:
        line, i = divmod(array, 4)
        keep = i == 0 and at < 2
        into = h_s.at[line] if keep else p_s.at[array]
        rows = slice(at * ROWS, (at + 1) * ROWS)
        into[rows, :HD] = (dk_s[pl.ds(row, ROWS), :] * SCALE).astype(into.dtype)
        into[rows, HD:] = dv_s[pl.ds(row, ROWS), :].astype(into.dtype)
        if at == 3:
            out = 5 * line + i
            near = [(h_s.at[line], out), (p_s.at[array, 2 * ROWS :], out + 1)]
            for source, n in near if i == 0 else [(p_s.at[array], out + 1)]:
                copies.append(pltpu.make_async_copy(source, part_refs[n], sems.at[n]))
                copies[-1].start()
    for copy in copies:
        copy.wait()


def attend(info, lengths, operands):
    bf16 = jnp.bfloat16
    side = jax.ShapeDtypeStruct((ROWS, WIDE), bf16)
    near = [
        jax.ShapeDtypeStruct((2 * ROWS, 2 * HD), jnp.float32),
        jax.ShapeDtypeStruct((2 * ROWS, 2 * HD), bf16),
    ]
    parts = near + [jax.ShapeDtypeStruct((4 * ROWS, 2 * HD), bf16)] * 3
    whole = pl.BlockSpec(memory_space=pltpu.VMEM)
    keys = 2 * SPAN
    return pl.pallas_call(
        attend_kernel,
        in_specs=[pl.BlockSpec(memory_space=pltpu.SMEM)] * 2 + [whole] * len(operands),
        out_specs=[whole] * 3 + [pl.BlockSpec(memory_space=pltpu.HBM)] * 10,
        out_shape=[side, side, jax.ShapeDtypeStruct((ROWS, 2 * WIDE), bf16)] + parts * 2,
        scratch_shapes=[
            pltpu.VMEM((2, LANES, HD), bf16),
            pltpu.VMEM((2, LANES, HD), bf16),
            pltpu.VMEM((keys, HD), bf16),
            pltpu.VMEM((keys, HD), bf16),
            pltpu.VMEM((keys, HD), jnp.float32),
            pltpu.VMEM((keys, HD), jnp.float32),
            pltpu.VMEM((REACH, LANES), jnp.float32),
            pltpu.VMEM((REACH, LANES), bf16),
            pltpu.VMEM((HD, LANES), jnp.float32),
            pltpu.VMEM((8, LANES), jnp.float32),
            pltpu.VMEM((8, LANES), jnp.float32),
            pltpu.VMEM((LANES, HD), bf16),
            pltpu.VMEM((LANES, HD), bf16),
            pltpu.VMEM((8, 4 * ROWS, 2 * HD), bf16),
            pltpu.VMEM((2, 2 * ROWS, 2 * HD), jnp.float32),
            pltpu.SemaphoreType.DMA((10,)),
        ],
        compiler_params=pltpu.CompilerParams(vmem_limit_bytes=48 * 1024 * 1024),
        name="attend",
    )(info, lengths, *operands)


def add(*terms):
    return sum(term.astype(jnp.float32) for term in terms).astype(jnp.bfloat16)


def body(queries, key_heads, value_heads, out_grad, lengths):
    count = lax.axis_size("stretch")
    stretch = lax.axis_index("stretch")
    h = lax.axis_index("head")
    core = lax.rem(stretch, 2)
    swap = [(s, s ^ 1) for s in range(count)]
    later = [(s, s + 2) for s in range(count - 2)]
    earlier = [(s + 2, s) for s in range(count - 2)]
    above, below = [
        [
            (s * RING + i, s * RING + (i + (1 if (s + i + turn) % 2 == 0 else -1)) % RING)
            for s in range(count)
            for i in range(RING)
        ]
        for turn in range(2)
    ]

    middle = 2 * ROWS

    def exchange(array, pairs):
        return lax.ppermute(array, ("stretch", "head"), pairs)

    def gather(held, neighbour):
        near = jnp.concatenate([held, neighbour], axis=0)
        second = exchange(near, below)
        third = exchange(second, above)
        return [near, second, third, exchange(third, below)]

    def scatter(here, near, second, third, fourth):
        third = add(third, exchange(fourth, below))
        second = add(second, exchange(third, above))
        come = exchange(second, below)
        return here + come[:middle].astype(jnp.float32), add(near, come[middle:])

    arrays = (queries, out_grad, key_heads, value_heads)

    def half(array, which, width):
        return lax.dynamic_slice_in_dim(array, which * width, width, axis=1)

    def pair(which):
        return jnp.concatenate([half(key_heads, which, HD), half(value_heads, which, HD)], axis=1)

    leaving = [half(array, 1 - core, array.shape[1] // 2) for array in arrays]
    come = lax.ppermute(jnp.concatenate(leaving, axis=1), "stretch", swap)
    own = jnp.concatenate([pair(core), come[:, 2 * WIDE :]], axis=0)
    past = lax.ppermute(own, "stretch", later)
    slant = [(a, b + 2 * RING) for a, b in above if b + 2 * RING < count * RING]
    info = jnp.stack([h, stretch]).astype(jnp.int32)
    operands = [queries, out_grad, come, *gather(own, exchange(own, above)), *gather(past, exchange(own, slant))]
    outs = attend(info, lengths, operands)
    def assemble(own, swapped):
        return jnp.where(
            core == 0,
            jnp.concatenate([own, swapped], axis=1),
            jnp.concatenate([swapped, own], axis=1),
        )

    past_here, past_near = scatter(*outs[8:13])
    here, near = scatter(*outs[3:8])
    past_sum = past_here + exchange(past_near, above).astype(jnp.float32)
    sent_back = lax.ppermute(past_sum.astype(jnp.bfloat16), "stretch", earlier)
    near, swapped = lax.optimization_barrier((near, outs[2]))
    here = here + exchange(near, above).astype(jnp.float32)
    swapped = lax.ppermute(swapped, "stretch", swap)
    attended = assemble(outs[0], swapped[:, :WIDE])
    query_grad = assemble(outs[1], swapped[:, WIDE:])
    summed = add(here, sent_back)
    mine, other = summed[:ROWS], lax.ppermute(summed[ROWS:], "stretch", swap)
    key_grad = assemble(mine[:, :HD], other[:, :HD])
    value_grad = assemble(mine[:, HD:], other[:, HD:])
    return attended, query_grad, key_grad, value_grad


def solution(mesh):
    spec = P(("dp", "stretch", "head"), None)
    return jax.shard_map(
        body,
        mesh=mesh,
        in_specs=(spec, spec, spec, spec, P("dp")),
        out_specs=(spec,) * 4,
        check_vma=False,
    )
```

```python
import jax
import jax.numpy as jnp
from jax import lax
from jax.experimental import pallas as pl
from jax.experimental.pallas import tpu as pltpu
from jax.sharding import PartitionSpec as P

HD = 128
GROUP = 8
ROWS = 128
WIDE = GROUP * HD
LANES = GROUP * ROWS
RING = 8
DISTANCES = ((0, 1), (-1, -2), (2, 3), (-3, -4))
REACH = 17 * ROWS
TILE = 8 * ROWS
SPAN = 2048
SCALE = HD**-0.5
EXP2 = SCALE * 1.4426950408889634
LOW = -1e30


def dot(x, y, cx, cy):
    return lax.dot_general(
        x, y, (((cx,), (cy,)), ((), ())), preferred_element_type=jnp.float32
    )


def attend_kernel(info, lengths, qo, go, come, *refs):
    kv_refs = refs[:8]
    att_own, dq_own, other = refs[8:11]
    part_refs = refs[11:21]
    q_s, g_s, k_s, v_s, dk_s, dv_s, s_s, w_s, o_s, top_s, sum_s, high_s, low_s, res_s, p_s, h_s, sems = refs[21:]
    h, core = info[0], lax.rem(info[1], 2)
    origin = (info[1] // 2 - 1) * SPAN
    base = pl.multiple_of(core * WIDE, WIDE)
    for n in range(GROUP):
        rows = slice(n * ROWS, (n + 1) * ROWS)
        q_s[0, rows, :] = qo[:, pl.ds(base + n * HD, HD)]
        g_s[0, rows, :] = go[:, pl.ds(base + n * HD, HD)]
        q_s[1, rows, :] = come[:, n * HD : (n + 1) * HD]
        g_s[1, rows, :] = come[:, WIDE + n * HD : WIDE + (n + 1) * HD]
    sign = 1 - 2 * lax.rem(h + core, 2)

    def row_of(distance, past, piece):
        j = lax.rem(h + sign * distance + RING, RING)
        side = core if piece == 0 else 1 - core
        chunk = j + 8 * side + (0 if past else 16)
        return pl.multiple_of(chunk * ROWS, ROWS)

    places = [
        (4 * past + i, 2 * at + piece, row_of(distance, past, piece))
        for past in range(2)
        for i, pair in enumerate(DISTANCES)
        for at, distance in enumerate(pair)
        for piece in range(2)
    ]
    for array, at, row in places:
        k_s[pl.ds(row, ROWS), :] = kv_refs[array][at * ROWS : (at + 1) * ROWS, :HD]
        v_s[pl.ds(row, ROWS), :] = kv_refs[array][at * ROWS : (at + 1) * ROWS, HD:]
    dk_s[...] = jnp.zeros_like(dk_s)
    dv_s[...] = jnp.zeros_like(dv_s)

    @pl.loop(0, 2)
    def _(slot):
        side = core + slot * (1 - 2 * core)
        first = SPAN + (h + 8 * side) * ROWS
        place = first + lax.broadcasted_iota(jnp.int32, (1, ROWS), 1)

        begin = reach = -origin
        start = jnp.full((1, ROWS), begin, jnp.int32)
        for i in range(lengths.shape[0] - 1):
            begin += lengths[i]
            reach = jnp.where(begin <= first, begin, reach)
            start = jnp.where(begin <= place, begin, start)
        low = reach // ROWS * ROWS
        chunks = (first + ROWS - low) // ROWS
        tiles = chunks // 8

        def over_keys(visit):
            def tile(b, carry):
                visit(pl.multiple_of(b * TILE, TILE), TILE)
                return carry

            lax.fori_loop(0, tiles, tile, 0)

            @pl.when(chunks % 8 >= 4)
            def _():
                visit(pl.multiple_of(tiles * TILE, TILE), 4 * ROWS)

            @pl.when(chunks % 4 >= 2)
            def _():
                visit(pl.multiple_of(chunks // 4 * 4 * ROWS, 4 * ROWS), 2 * ROWS)

            @pl.when(chunks % 2 == 1)
            def _():
                visit(pl.multiple_of((chunks - 1) * ROWS, ROWS), ROWS)

        start = jnp.concatenate([start] * GROUP, axis=1)
        place = jnp.concatenate([place] * GROUP, axis=1)

        def scores(at, size):
            row = pl.multiple_of(low + at, ROWS)
            raw = dot(k_s[pl.ds(row, size), :], q_s[slot], 1, 1)
            key_place = row + lax.broadcasted_iota(jnp.int32, (size, LANES), 0)
            raw = jnp.where((key_place >= start) & (key_place <= place), raw, LOW)
            s_s[pl.ds(at, size), :] = raw
            top_s[...] = jnp.maximum(top_s[...], jnp.max(raw.reshape(size // 8, 8, LANES), axis=0))

        top_s[...] = jnp.full_like(top_s, LOW)
        over_keys(scores)
        top = jnp.max(top_s[...], axis=0, keepdims=True)
        sum_s[...] = jnp.zeros_like(sum_s)
        o_s[...] = jnp.zeros_like(o_s)

        def forward(at, size):
            row = pl.multiple_of(low + at, ROWS)
            weight = jnp.exp2((s_s[pl.ds(at, size), :] - top) * EXP2)
            rounded = weight.astype(jnp.bfloat16)
            w_s[pl.ds(at, size), :] = rounded
            o_s[...] += dot(v_s[pl.ds(row, size), :], rounded, 0, 0)
            sum_s[...] += jnp.sum(weight.reshape(size // 8, 8, LANES), axis=0)

        over_keys(forward)
        inverse = 1.0 / jnp.sum(sum_s[...], axis=0, keepdims=True)
        wide = jnp.broadcast_to(inverse, (8, LANES))
        for n in range(GROUP):
            cols = slice(n * HD, (n + 1) * HD)
            rows = slice(n * ROWS, (n + 1) * ROWS)
            att = jnp.transpose((o_s[:, rows] * inverse[:, rows]).astype(jnp.bfloat16))
            res_s[slot, :, cols] = att
            column = jnp.transpose(wide[:, rows])[:, :1]
            scaled = (g_s[slot, rows, :].astype(jnp.float32) * column).astype(jnp.bfloat16)
            g_s[slot, rows, :] = scaled
            product = att.astype(jnp.float32) * scaled.astype(jnp.float32)
            high_s[rows, :] = product.astype(jnp.bfloat16)
            low_s[rows, :] = (product - product.astype(jnp.bfloat16).astype(jnp.float32)).astype(jnp.bfloat16)
        ones = jnp.ones((8, HD), jnp.bfloat16)
        correction = (dot(ones, high_s[...], 1, 1) + dot(ones, low_s[...], 1, 1))[:1]
        o_s[...] = jnp.zeros_like(o_s)

        def backward(at, size):
            keys = pl.ds(pl.multiple_of(low + at, ROWS), size)
            weight = w_s[pl.ds(at, size), :]
            weight_grad = dot(v_s[keys, :], g_s[slot], 1, 1)
            score_grad = weight.astype(jnp.float32) * (weight_grad - correction)
            score_grad = score_grad.astype(jnp.bfloat16)
            dv_s[keys, :] += dot(weight, g_s[slot], 1, 0)
            dk_s[keys, :] += dot(score_grad, q_s[slot], 1, 0)
            o_s[...] += dot(k_s[keys, :], score_grad, 0, 0)

        over_keys(backward)
        for n in range(GROUP):
            rows = slice(n * ROWS, (n + 1) * ROWS)
            query_grad = jnp.transpose((o_s[:, rows] * SCALE).astype(jnp.bfloat16))
            res_s[slot, :, WIDE + n * HD : WIDE + (n + 1) * HD] = query_grad

    att_own[...] = res_s[0, :, :WIDE]
    dq_own[...] = res_s[0, :, WIDE:]
    other[...] = res_s[1]

    copies = []
    for array, at, row in places:
        line, i = divmod(array, 4)
        keep = i == 0 and at < 2
        into = h_s.at[line] if keep else p_s.at[array]
        rows = slice(at * ROWS, (at + 1) * ROWS)
        into[rows, :HD] = (dk_s[pl.ds(row, ROWS), :] * SCALE).astype(into.dtype)
        into[rows, HD:] = dv_s[pl.ds(row, ROWS), :].astype(into.dtype)
        if at == 3:
            out = 5 * line + i
            near = [(h_s.at[line], out), (p_s.at[array, 2 * ROWS :], out + 1)]
            for source, n in near if i == 0 else [(p_s.at[array], out + 1)]:
                copies.append(pltpu.make_async_copy(source, part_refs[n], sems.at[n]))
                copies[-1].start()
    for copy in copies:
        copy.wait()


def attend(info, lengths, operands):
    bf16 = jnp.bfloat16
    side = jax.ShapeDtypeStruct((ROWS, WIDE), bf16)
    near = [
        jax.ShapeDtypeStruct((2 * ROWS, 2 * HD), jnp.float32),
        jax.ShapeDtypeStruct((2 * ROWS, 2 * HD), bf16),
    ]
    parts = near + [jax.ShapeDtypeStruct((4 * ROWS, 2 * HD), bf16)] * 3
    whole = pl.BlockSpec(memory_space=pltpu.VMEM)
    keys = 2 * SPAN
    return pl.pallas_call(
        attend_kernel,
        in_specs=[pl.BlockSpec(memory_space=pltpu.SMEM)] * 2 + [whole] * len(operands),
        out_specs=[whole] * 3 + [pl.BlockSpec(memory_space=pltpu.HBM)] * 10,
        out_shape=[side, side, jax.ShapeDtypeStruct((ROWS, 2 * WIDE), bf16)] + parts * 2,
        scratch_shapes=[
            pltpu.VMEM((2, LANES, HD), bf16),
            pltpu.VMEM((2, LANES, HD), bf16),
            pltpu.VMEM((keys, HD), bf16),
            pltpu.VMEM((keys, HD), bf16),
            pltpu.VMEM((keys, HD), jnp.float32),
            pltpu.VMEM((keys, HD), jnp.float32),
            pltpu.VMEM((REACH, LANES), jnp.float32),
            pltpu.VMEM((REACH, LANES), bf16),
            pltpu.VMEM((HD, LANES), jnp.float32),
            pltpu.VMEM((8, LANES), jnp.float32),
            pltpu.VMEM((8, LANES), jnp.float32),
            pltpu.VMEM((LANES, HD), bf16),
            pltpu.VMEM((LANES, HD), bf16),
            pltpu.VMEM((2, ROWS, 2 * WIDE), bf16),
            pltpu.VMEM((8, 4 * ROWS, 2 * HD), bf16),
            pltpu.VMEM((2, 2 * ROWS, 2 * HD), jnp.float32),
            pltpu.SemaphoreType.DMA((10,)),
        ],
        compiler_params=pltpu.CompilerParams(vmem_limit_bytes=48 * 1024 * 1024),
        name="attend",
    )(info, lengths, *operands)


def join_kernel(info, att, dq, come, here, sent, other, att_out, dq_out, key_out, value_out):
    core = lax.rem(info[1], 2)
    own = pl.multiple_of(core * WIDE, WIDE)
    far = pl.multiple_of((1 - core) * WIDE, WIDE)
    att_out[:, pl.ds(own, WIDE)] = att[...]
    att_out[:, pl.ds(far, WIDE)] = come[:, :WIDE]
    dq_out[:, pl.ds(own, WIDE)] = dq[...]
    dq_out[:, pl.ds(far, WIDE)] = come[:, WIDE:]
    mine = (here[...] + sent[...].astype(jnp.float32)).astype(jnp.bfloat16)
    own = pl.multiple_of(core * HD, HD)
    far = pl.multiple_of((1 - core) * HD, HD)
    key_out[:, pl.ds(own, HD)] = mine[:, :HD]
    key_out[:, pl.ds(far, HD)] = other[:, :HD]
    value_out[:, pl.ds(own, HD)] = mine[:, HD:]
    value_out[:, pl.ds(far, HD)] = other[:, HD:]


def join(info, operands):
    whole = pl.BlockSpec(memory_space=pltpu.VMEM)
    long = jax.ShapeDtypeStruct((ROWS, 2 * WIDE), jnp.bfloat16)
    short = jax.ShapeDtypeStruct((ROWS, 2 * HD), jnp.bfloat16)
    return pl.pallas_call(
        join_kernel,
        in_specs=[pl.BlockSpec(memory_space=pltpu.SMEM)] + [whole] * len(operands),
        out_specs=[whole] * 4,
        out_shape=[long, long, short, short],
        compiler_params=pltpu.CompilerParams(vmem_limit_bytes=16 * 1024 * 1024),
        name="join",
    )(info, *operands)


def add(*terms):
    return sum(term.astype(jnp.float32) for term in terms).astype(jnp.bfloat16)


def body(queries, key_heads, value_heads, out_grad, lengths):
    count = lax.axis_size("stretch")
    stretch = lax.axis_index("stretch")
    h = lax.axis_index("head")
    core = lax.rem(stretch, 2)
    swap = [(s, s ^ 1) for s in range(count)]
    later = [(s, s + 2) for s in range(count - 2)]
    earlier = [(s + 2, s) for s in range(count - 2)]
    above, below = [
        [
            (s * RING + i, s * RING + (i + (1 if (s + i + turn) % 2 == 0 else -1)) % RING)
            for s in range(count)
            for i in range(RING)
        ]
        for turn in range(2)
    ]

    middle = 2 * ROWS

    def exchange(array, pairs):
        return lax.ppermute(array, ("stretch", "head"), pairs)

    def gather(held, neighbour):
        near = jnp.concatenate([held, neighbour], axis=0)
        second = exchange(near, below)
        third = exchange(second, above)
        return [near, second, third, exchange(third, below)]

    def scatter(here, near, second, third, fourth):
        third = add(third, exchange(fourth, below))
        second = add(second, exchange(third, above))
        come = exchange(second, below)
        return here + come[:middle].astype(jnp.float32), add(near, come[middle:])

    arrays = (queries, out_grad, key_heads, value_heads)

    def half(array, which, width):
        return lax.dynamic_slice_in_dim(array, which * width, width, axis=1)

    def pair(which):
        return jnp.concatenate([half(key_heads, which, HD), half(value_heads, which, HD)], axis=1)

    leaving = [half(array, 1 - core, array.shape[1] // 2) for array in arrays]
    come = lax.ppermute(jnp.concatenate(leaving, axis=1), "stretch", swap)
    own = jnp.concatenate([pair(core), come[:, 2 * WIDE :]], axis=0)
    past = lax.ppermute(own, "stretch", later)
    slant = [(a, b + 2 * RING) for a, b in above if b + 2 * RING < count * RING]
    slanted = exchange(own, slant)
    info = jnp.stack([h, stretch]).astype(jnp.int32)
    operands = [queries, out_grad, come, *gather(own, exchange(own, above)), *gather(past, slanted)]
    outs = attend(info, lengths, operands)
    past_here, past_near = scatter(*outs[8:13])
    here, near = scatter(*outs[3:8])
    past_sum = past_here + exchange(past_near, above).astype(jnp.float32)
    sent_back = lax.ppermute(past_sum.astype(jnp.bfloat16), "stretch", earlier)
    near, swapped = lax.optimization_barrier((near, outs[2]))
    here = here + exchange(near, above).astype(jnp.float32)
    swapped = lax.ppermute(swapped, "stretch", swap)
    other = lax.ppermute(add(here[ROWS:], sent_back[ROWS:]), "stretch", swap)
    return join(info, [outs[0], outs[1], swapped, here[:ROWS], sent_back[:ROWS], other])


def solution(mesh):
    spec = P(("dp", "stretch", "head"), None)
    return jax.shard_map(
        body,
        mesh=mesh,
        in_specs=(spec, spec, spec, spec, P("dp")),
        out_specs=(spec,) * 4,
        check_vma=False,
    )
```

```python
import jax
import jax.numpy as jnp
from jax import lax
from jax.experimental import pallas as pl
from jax.experimental.pallas import tpu as pltpu
from jax.sharding import PartitionSpec as P

HD = 128
GROUP = 8
ROWS = 128
WIDE = GROUP * HD
LANES = GROUP * ROWS
RING = 8
DISTANCES = ((0, 1), (-1, -2), (2, 3), (-3, -4))
REACH = 17 * ROWS
TILE = 8 * ROWS
SPAN = 2048
SCALE = HD**-0.5
EXP2 = SCALE * 1.4426950408889634
LOW = -1e30


def dot(x, y, cx, cy):
    return lax.dot_general(
        x, y, (((cx,), (cy,)), ((), ())), preferred_element_type=jnp.float32
    )


def attend_kernel(info, lengths, qo, go, come, *refs):
    kv_refs = refs[:8]
    att_own, dq_own, other = refs[8:11]
    part_refs = refs[11:21]
    q_s, g_s, k_s, v_s, dk_s, dv_s, s_s, w_s, o_s, top_s, sum_s, high_s, low_s, res_s = refs[21:]
    h, core = info[0], lax.rem(info[1], 2)
    origin = (info[1] // 2 - 1) * SPAN
    base = pl.multiple_of(core * WIDE, WIDE)
    for n in range(GROUP):
        rows = slice(n * ROWS, (n + 1) * ROWS)
        q_s[0, rows, :] = qo[:, pl.ds(base + n * HD, HD)]
        g_s[0, rows, :] = go[:, pl.ds(base + n * HD, HD)]
        q_s[1, rows, :] = come[:, n * HD : (n + 1) * HD]
        g_s[1, rows, :] = come[:, WIDE + n * HD : WIDE + (n + 1) * HD]
    sign = 1 - 2 * lax.rem(h + core, 2)

    def row_of(distance, past, piece):
        j = lax.rem(h + sign * distance + RING, RING)
        side = core if piece == 0 else 1 - core
        chunk = j + 8 * side + (0 if past else 16)
        return pl.multiple_of(chunk * ROWS, ROWS)

    places = [
        (4 * past + i, 2 * at + piece, row_of(distance, past, piece))
        for past in range(2)
        for i, pair in enumerate(DISTANCES)
        for at, distance in enumerate(pair)
        for piece in range(2)
    ]
    for array, at, row in places:
        k_s[pl.ds(row, ROWS), :] = kv_refs[array][at * ROWS : (at + 1) * ROWS, :HD]
        v_s[pl.ds(row, ROWS), :] = kv_refs[array][at * ROWS : (at + 1) * ROWS, HD:]
    dk_s[...] = jnp.zeros_like(dk_s)
    dv_s[...] = jnp.zeros_like(dv_s)

    @pl.loop(0, 2)
    def _(slot):
        side = core + slot * (1 - 2 * core)
        first = SPAN + (h + 8 * side) * ROWS
        place = first + lax.broadcasted_iota(jnp.int32, (1, ROWS), 1)

        begin = reach = -origin
        start = jnp.full((1, ROWS), begin, jnp.int32)
        for i in range(lengths.shape[0] - 1):
            begin += lengths[i]
            reach = jnp.where(begin <= first, begin, reach)
            start = jnp.where(begin <= place, begin, start)
        low = reach // ROWS * ROWS
        chunks = (first + ROWS - low) // ROWS
        tiles = chunks // 8

        def over_keys(visit):
            def tile(b, carry):
                visit(pl.multiple_of(b * TILE, TILE), TILE)
                return carry

            lax.fori_loop(0, tiles, tile, 0)

            @pl.when(chunks % 8 >= 4)
            def _():
                visit(pl.multiple_of(tiles * TILE, TILE), 4 * ROWS)

            @pl.when(chunks % 4 >= 2)
            def _():
                visit(pl.multiple_of(chunks // 4 * 4 * ROWS, 4 * ROWS), 2 * ROWS)

            @pl.when(chunks % 2 == 1)
            def _():
                visit(pl.multiple_of((chunks - 1) * ROWS, ROWS), ROWS)

        start = jnp.concatenate([start] * GROUP, axis=1)
        place = jnp.concatenate([place] * GROUP, axis=1)

        def scores(at, size):
            row = pl.multiple_of(low + at, ROWS)
            raw = dot(k_s[pl.ds(row, size), :], q_s[slot], 1, 1)
            key_place = row + lax.broadcasted_iota(jnp.int32, (size, LANES), 0)
            raw = jnp.where((key_place >= start) & (key_place <= place), raw, LOW)
            s_s[pl.ds(at, size), :] = raw
            top_s[...] = jnp.maximum(top_s[...], jnp.max(raw.reshape(size // 8, 8, LANES), axis=0))

        top_s[...] = jnp.full_like(top_s, LOW)
        over_keys(scores)
        top = jnp.max(top_s[...], axis=0, keepdims=True)
        sum_s[...] = jnp.zeros_like(sum_s)
        o_s[...] = jnp.zeros_like(o_s)

        def forward(at, size):
            row = pl.multiple_of(low + at, ROWS)
            weight = jnp.exp2((s_s[pl.ds(at, size), :] - top) * EXP2)
            rounded = weight.astype(jnp.bfloat16)
            w_s[pl.ds(at, size), :] = rounded
            o_s[...] += dot(v_s[pl.ds(row, size), :], rounded, 0, 0)
            sum_s[...] += jnp.sum(weight.reshape(size // 8, 8, LANES), axis=0)

        over_keys(forward)
        inverse = 1.0 / jnp.sum(sum_s[...], axis=0, keepdims=True)
        wide = jnp.broadcast_to(inverse, (8, LANES))
        for n in range(GROUP):
            cols = slice(n * HD, (n + 1) * HD)
            rows = slice(n * ROWS, (n + 1) * ROWS)
            att = jnp.transpose((o_s[:, rows] * inverse[:, rows]).astype(jnp.bfloat16))
            res_s[slot, :, cols] = att
            column = jnp.transpose(wide[:, rows])[:, :1]
            scaled = (g_s[slot, rows, :].astype(jnp.float32) * column).astype(jnp.bfloat16)
            g_s[slot, rows, :] = scaled
            product = att.astype(jnp.float32) * scaled.astype(jnp.float32)
            high_s[rows, :] = product.astype(jnp.bfloat16)
            low_s[rows, :] = (product - product.astype(jnp.bfloat16).astype(jnp.float32)).astype(jnp.bfloat16)
        ones = jnp.ones((8, HD), jnp.bfloat16)
        correction = (dot(ones, high_s[...], 1, 1) + dot(ones, low_s[...], 1, 1))[:1]
        o_s[...] = jnp.zeros_like(o_s)

        def backward(at, size):
            keys = pl.ds(pl.multiple_of(low + at, ROWS), size)
            weight = w_s[pl.ds(at, size), :]
            weight_grad = dot(v_s[keys, :], g_s[slot], 1, 1)
            score_grad = weight.astype(jnp.float32) * (weight_grad - correction)
            score_grad = score_grad.astype(jnp.bfloat16)
            dv_s[keys, :] += dot(weight, g_s[slot], 1, 0)
            dk_s[keys, :] += dot(score_grad, q_s[slot], 1, 0)
            o_s[...] += dot(k_s[keys, :], score_grad, 0, 0)

        over_keys(backward)
        for n in range(GROUP):
            rows = slice(n * ROWS, (n + 1) * ROWS)
            query_grad = jnp.transpose((o_s[:, rows] * SCALE).astype(jnp.bfloat16))
            res_s[slot, :, WIDE + n * HD : WIDE + (n + 1) * HD] = query_grad

    att_own[...] = res_s[0, :, :WIDE]
    dq_own[...] = res_s[0, :, WIDE:]
    other[...] = res_s[1]

    for array, at, row in places:
        line, i = divmod(array, 4)
        part = part_refs[5 * line + i + (0 if i == 0 and at < 2 else 1)]
        at = at % 2 if i == 0 else at
        rows = slice(at * ROWS, (at + 1) * ROWS)
        part[rows, :HD] = (dk_s[pl.ds(row, ROWS), :] * SCALE).astype(part.dtype)
        part[rows, HD:] = dv_s[pl.ds(row, ROWS), :].astype(part.dtype)


def attend(info, lengths, operands):
    bf16 = jnp.bfloat16
    side = jax.ShapeDtypeStruct((ROWS, WIDE), bf16)
    near = [
        jax.ShapeDtypeStruct((2 * ROWS, 2 * HD), jnp.float32),
        jax.ShapeDtypeStruct((2 * ROWS, 2 * HD), bf16),
    ]
    parts = near + [jax.ShapeDtypeStruct((4 * ROWS, 2 * HD), bf16)] * 3
    whole = pl.BlockSpec(memory_space=pltpu.VMEM)
    keys = 2 * SPAN
    return pl.pallas_call(
        attend_kernel,
        in_specs=[pl.BlockSpec(memory_space=pltpu.SMEM)] * 2 + [whole] * len(operands),
        out_specs=[whole] * 13,
        out_shape=[side, side, jax.ShapeDtypeStruct((ROWS, 2 * WIDE), bf16)] + parts * 2,
        scratch_shapes=[
            pltpu.VMEM((2, LANES, HD), bf16),
            pltpu.VMEM((2, LANES, HD), bf16),
            pltpu.VMEM((keys, HD), bf16),
            pltpu.VMEM((keys, HD), bf16),
            pltpu.VMEM((keys, HD), jnp.float32),
            pltpu.VMEM((keys, HD), jnp.float32),
            pltpu.VMEM((REACH, LANES), jnp.float32),
            pltpu.VMEM((REACH, LANES), bf16),
            pltpu.VMEM((HD, LANES), jnp.float32),
            pltpu.VMEM((8, LANES), jnp.float32),
            pltpu.VMEM((8, LANES), jnp.float32),
            pltpu.VMEM((LANES, HD), bf16),
            pltpu.VMEM((LANES, HD), bf16),
            pltpu.VMEM((2, ROWS, 2 * WIDE), bf16),
        ],
        compiler_params=pltpu.CompilerParams(vmem_limit_bytes=48 * 1024 * 1024),
        name="attend",
    )(info, lengths, *operands)


def join_kernel(info, att, dq, come, here, sent, other, att_out, dq_out, key_out, value_out):
    core = lax.rem(info[1], 2)
    own = pl.multiple_of(core * WIDE, WIDE)
    far = pl.multiple_of((1 - core) * WIDE, WIDE)
    att_out[:, pl.ds(own, WIDE)] = att[...]
    att_out[:, pl.ds(far, WIDE)] = come[:, :WIDE]
    dq_out[:, pl.ds(own, WIDE)] = dq[...]
    dq_out[:, pl.ds(far, WIDE)] = come[:, WIDE:]
    mine = (here[...] + sent[...].astype(jnp.float32)).astype(jnp.bfloat16)
    own = pl.multiple_of(core * HD, HD)
    far = pl.multiple_of((1 - core) * HD, HD)
    key_out[:, pl.ds(own, HD)] = mine[:, :HD]
    key_out[:, pl.ds(far, HD)] = other[:, :HD]
    value_out[:, pl.ds(own, HD)] = mine[:, HD:]
    value_out[:, pl.ds(far, HD)] = other[:, HD:]


def join(info, operands):
    whole = pl.BlockSpec(memory_space=pltpu.VMEM)
    long = jax.ShapeDtypeStruct((ROWS, 2 * WIDE), jnp.bfloat16)
    short = jax.ShapeDtypeStruct((ROWS, 2 * HD), jnp.bfloat16)
    return pl.pallas_call(
        join_kernel,
        in_specs=[pl.BlockSpec(memory_space=pltpu.SMEM)] + [whole] * len(operands),
        out_specs=[whole] * 4,
        out_shape=[long, long, short, short],
        compiler_params=pltpu.CompilerParams(vmem_limit_bytes=16 * 1024 * 1024),
        name="join",
    )(info, *operands)


def add(*terms):
    return sum(term.astype(jnp.float32) for term in terms).astype(jnp.bfloat16)


def body(queries, key_heads, value_heads, out_grad, lengths):
    count = lax.axis_size("stretch")
    stretch = lax.axis_index("stretch")
    h = lax.axis_index("head")
    core = lax.rem(stretch, 2)
    swap = [(s, s ^ 1) for s in range(count)]
    later = [(s, s + 2) for s in range(count - 2)]
    earlier = [(s + 2, s) for s in range(count - 2)]
    above, below = [
        [
            (s * RING + i, s * RING + (i + (1 if (s + i + turn) % 2 == 0 else -1)) % RING)
            for s in range(count)
            for i in range(RING)
        ]
        for turn in range(2)
    ]

    middle = 2 * ROWS

    def exchange(array, pairs):
        return lax.ppermute(array, ("stretch", "head"), pairs)

    def gather(held, neighbour):
        near = jnp.concatenate([held, neighbour], axis=0)
        second = exchange(near, below)
        third = exchange(second, above)
        return [near, second, third, exchange(third, below)]

    def scatter(here, near, second, third, fourth):
        third = add(third, exchange(fourth, below))
        second = add(second, exchange(third, above))
        come = exchange(second, below)
        return here + come[:middle].astype(jnp.float32), add(near, come[middle:])

    def half(array, which, width):
        return lax.dynamic_slice_in_dim(array, which * width, width, axis=1)

    def pair(which):
        return jnp.concatenate([half(key_heads, which, HD), half(value_heads, which, HD)], axis=1)

    own = jnp.concatenate([pair(core), lax.ppermute(pair(1 - core), "stretch", swap)], axis=0)
    leaving = [half(array, 1 - core, WIDE) for array in (queries, out_grad)]
    come = lax.ppermute(jnp.concatenate(leaving, axis=1), "stretch", swap)
    past = lax.ppermute(own, "stretch", later)
    slant = [(a, b + 2 * RING) for a, b in above if b + 2 * RING < count * RING]
    slanted = exchange(own, slant)
    info = jnp.stack([h, stretch]).astype(jnp.int32)
    operands = [queries, out_grad, come, *gather(own, exchange(own, above)), *gather(past, slanted)]
    outs = attend(info, lengths, operands)
    past_here, past_near = scatter(*outs[8:13])
    here, near = scatter(*outs[3:8])
    past_sum = past_here + exchange(past_near, above).astype(jnp.float32)
    sent_back = lax.ppermute(past_sum.astype(jnp.bfloat16), "stretch", earlier)
    near, swapped = lax.optimization_barrier((near, outs[2]))
    here = here + exchange(near, above).astype(jnp.float32)
    swapped = lax.ppermute(swapped, "stretch", swap)
    other = lax.ppermute(add(here[ROWS:], sent_back[ROWS:]), "stretch", swap)
    return join(info, [outs[0], outs[1], swapped, here[:ROWS], sent_back[:ROWS], other])


def solution(mesh):
    spec = P(("dp", "stretch", "head"), None)
    return jax.shard_map(
        body,
        mesh=mesh,
        in_specs=(spec, spec, spec, spec, P("dp")),
        out_specs=(spec,) * 4,
        check_vma=False,
    )
```

```python
import jax
import jax.numpy as jnp
from jax import lax
from jax.experimental import pallas as pl
from jax.experimental.pallas import tpu as pltpu
from jax.sharding import PartitionSpec as P

HD = 128
GROUP = 8
ROWS = 128
WIDE = GROUP * HD
LANES = GROUP * ROWS
RING = 8
DISTANCES = ((0, 1), (-1, -2), (2, 3), (-3, -4))
REACH = 17 * ROWS
TILE = 8 * ROWS
SPAN = 2048
SCALE = HD**-0.5
EXP2 = SCALE * 1.4426950408889634
LOW = -1e30


def dot(x, y, cx, cy):
    return lax.dot_general(
        x, y, (((cx,), (cy,)), ((), ())), preferred_element_type=jnp.float32
    )


def attend_kernel(info, lengths, qo, go, come, *refs):
    kv_refs = refs[:8]
    att_own, dq_own, other = refs[8:11]
    part_refs = refs[11:21]
    q_s, g_s, k_s, v_s, dk_s, dv_s, s_s, w_s, o_s, top_s, sum_s, high_s, low_s, res_s = refs[21:]
    h, core = info[0], lax.rem(info[1], 2)
    origin = (info[1] // 2 - 1) * SPAN
    base = pl.multiple_of(core * WIDE, WIDE)
    for n in range(GROUP):
        rows = slice(n * ROWS, (n + 1) * ROWS)
        q_s[0, rows, :] = qo[:, pl.ds(base + n * HD, HD)]
        g_s[0, rows, :] = go[:, pl.ds(base + n * HD, HD)]
        q_s[1, rows, :] = come[:, n * HD : (n + 1) * HD]
        g_s[1, rows, :] = come[:, WIDE + n * HD : WIDE + (n + 1) * HD]
    sign = 1 - 2 * lax.rem(h + core, 2)

    def row_of(distance, past, piece):
        j = lax.rem(h + sign * distance + RING, RING)
        side = core if piece == 0 else 1 - core
        chunk = j + 8 * side + (0 if past else 16)
        return pl.multiple_of(chunk * ROWS, ROWS)

    places = [
        (4 * past + i, 2 * at + piece, row_of(distance, past, piece))
        for past in range(2)
        for i, pair in enumerate(DISTANCES)
        for at, distance in enumerate(pair)
        for piece in range(2)
    ]
    for array, at, row in places:
        k_s[pl.ds(row, ROWS), :] = kv_refs[array][at * ROWS : (at + 1) * ROWS, :HD]
        v_s[pl.ds(row, ROWS), :] = kv_refs[array][at * ROWS : (at + 1) * ROWS, HD:]
    dk_s[...] = jnp.zeros_like(dk_s)
    dv_s[...] = jnp.zeros_like(dv_s)

    @pl.loop(0, 2)
    def _(slot):
        side = core + slot * (1 - 2 * core)
        first = SPAN + (h + 8 * side) * ROWS
        place = first + lax.broadcasted_iota(jnp.int32, (1, ROWS), 1)

        begin = reach = -origin
        start = jnp.full((1, ROWS), begin, jnp.int32)
        for i in range(lengths.shape[0] - 1):
            begin += lengths[i]
            reach = jnp.where(begin <= first, begin, reach)
            start = jnp.where(begin <= place, begin, start)
        low = reach // ROWS * ROWS
        chunks = (first + ROWS - low) // ROWS
        tiles = chunks // 8

        def over_keys(visit):
            def tile(b, carry):
                visit(pl.multiple_of(b * TILE, TILE), TILE)
                return carry

            lax.fori_loop(0, tiles, tile, 0)

            @pl.when(chunks % 8 >= 4)
            def _():
                visit(pl.multiple_of(tiles * TILE, TILE), 4 * ROWS)

            @pl.when(chunks % 4 >= 2)
            def _():
                visit(pl.multiple_of(chunks // 4 * 4 * ROWS, 4 * ROWS), 2 * ROWS)

            @pl.when(chunks % 2 == 1)
            def _():
                visit(pl.multiple_of((chunks - 1) * ROWS, ROWS), ROWS)

        start = jnp.concatenate([start] * GROUP, axis=1)
        place = jnp.concatenate([place] * GROUP, axis=1)

        def scores(at, size):
            row = pl.multiple_of(low + at, ROWS)
            raw = dot(k_s[pl.ds(row, size), :], q_s[slot], 1, 1)
            key_place = row + lax.broadcasted_iota(jnp.int32, (size, LANES), 0)
            raw = jnp.where((key_place >= start) & (key_place <= place), raw, LOW)
            s_s[pl.ds(at, size), :] = raw
            top_s[...] = jnp.maximum(top_s[...], jnp.max(raw.reshape(size // 8, 8, LANES), axis=0))

        top_s[...] = jnp.full_like(top_s, LOW)
        over_keys(scores)
        top = jnp.max(top_s[...], axis=0, keepdims=True)
        sum_s[...] = jnp.zeros_like(sum_s)
        o_s[...] = jnp.zeros_like(o_s)

        def forward(at, size):
            row = pl.multiple_of(low + at, ROWS)
            weight = jnp.exp2((s_s[pl.ds(at, size), :] - top) * EXP2)
            rounded = weight.astype(jnp.bfloat16)
            w_s[pl.ds(at, size), :] = rounded
            o_s[...] += dot(v_s[pl.ds(row, size), :], rounded, 0, 0)
            sum_s[...] += jnp.sum(weight.reshape(size // 8, 8, LANES), axis=0)

        over_keys(forward)
        inverse = 1.0 / jnp.sum(sum_s[...], axis=0, keepdims=True)
        wide = jnp.broadcast_to(inverse, (8, LANES))
        for n in range(GROUP):
            cols = slice(n * HD, (n + 1) * HD)
            rows = slice(n * ROWS, (n + 1) * ROWS)
            att = jnp.transpose((o_s[:, rows] * inverse[:, rows]).astype(jnp.bfloat16))
            res_s[slot, :, cols] = att
            column = jnp.transpose(wide[:, rows])[:, :1]
            scaled = (g_s[slot, rows, :].astype(jnp.float32) * column).astype(jnp.bfloat16)
            g_s[slot, rows, :] = scaled
            product = att.astype(jnp.float32) * scaled.astype(jnp.float32)
            high_s[rows, :] = product.astype(jnp.bfloat16)
            low_s[rows, :] = (product - product.astype(jnp.bfloat16).astype(jnp.float32)).astype(jnp.bfloat16)
        ones = jnp.ones((8, HD), jnp.bfloat16)
        correction = (dot(ones, high_s[...], 1, 1) + dot(ones, low_s[...], 1, 1))[:1]
        o_s[...] = jnp.zeros_like(o_s)

        def backward(at, size):
            keys = pl.ds(pl.multiple_of(low + at, ROWS), size)
            weight = w_s[pl.ds(at, size), :]
            weight_grad = dot(v_s[keys, :], g_s[slot], 1, 1)
            score_grad = weight.astype(jnp.float32) * (weight_grad - correction)
            score_grad = score_grad.astype(jnp.bfloat16)
            dv_s[keys, :] += dot(weight, g_s[slot], 1, 0)
            dk_s[keys, :] += dot(score_grad, q_s[slot], 1, 0)
            o_s[...] += dot(k_s[keys, :], score_grad, 0, 0)

        over_keys(backward)
        for n in range(GROUP):
            rows = slice(n * ROWS, (n + 1) * ROWS)
            query_grad = jnp.transpose((o_s[:, rows] * SCALE).astype(jnp.bfloat16))
            res_s[slot, :, WIDE + n * HD : WIDE + (n + 1) * HD] = query_grad

    att_own[...] = res_s[0, :, :WIDE]
    dq_own[...] = res_s[0, :, WIDE:]
    other[...] = res_s[1]

    for array, at, row in places:
        line, i = divmod(array, 4)
        part = part_refs[5 * line + i + (0 if i == 0 and at < 2 else 1)]
        at = at % 2 if i == 0 else at
        rows = slice(at * ROWS, (at + 1) * ROWS)
        part[rows, :HD] = (dk_s[pl.ds(row, ROWS), :] * SCALE).astype(part.dtype)
        part[rows, HD:] = dv_s[pl.ds(row, ROWS), :].astype(part.dtype)


def attend(info, lengths, operands):
    bf16 = jnp.bfloat16
    side = jax.ShapeDtypeStruct((ROWS, WIDE), bf16)
    near = [
        jax.ShapeDtypeStruct((2 * ROWS, 2 * HD), jnp.float32),
        jax.ShapeDtypeStruct((2 * ROWS, 2 * HD), bf16),
    ]
    parts = near + [jax.ShapeDtypeStruct((4 * ROWS, 2 * HD), bf16)] * 3
    whole = pl.BlockSpec(memory_space=pltpu.VMEM)
    keys = 2 * SPAN
    return pl.pallas_call(
        attend_kernel,
        in_specs=[pl.BlockSpec(memory_space=pltpu.SMEM)] * 2 + [whole] * len(operands),
        out_specs=[whole] * 13,
        out_shape=[side, side, jax.ShapeDtypeStruct((ROWS, 2 * WIDE), bf16)] + parts * 2,
        scratch_shapes=[
            pltpu.VMEM((2, LANES, HD), bf16),
            pltpu.VMEM((2, LANES, HD), bf16),
            pltpu.VMEM((keys, HD), bf16),
            pltpu.VMEM((keys, HD), bf16),
            pltpu.VMEM((keys, HD), jnp.float32),
            pltpu.VMEM((keys, HD), jnp.float32),
            pltpu.VMEM((REACH, LANES), jnp.float32),
            pltpu.VMEM((REACH, LANES), bf16),
            pltpu.VMEM((HD, LANES), jnp.float32),
            pltpu.VMEM((8, LANES), jnp.float32),
            pltpu.VMEM((8, LANES), jnp.float32),
            pltpu.VMEM((LANES, HD), bf16),
            pltpu.VMEM((LANES, HD), bf16),
            pltpu.VMEM((2, ROWS, 2 * WIDE), bf16),
        ],
        compiler_params=pltpu.CompilerParams(vmem_limit_bytes=48 * 1024 * 1024),
        name="attend",
    )(info, lengths, *operands)


def place_kernel(info, att, dq, come, att_out, dq_out):
    core = lax.rem(info[1], 2)
    own = pl.multiple_of(core * WIDE, WIDE)
    far = pl.multiple_of((1 - core) * WIDE, WIDE)
    att_out[:, pl.ds(own, WIDE)] = att[...]
    att_out[:, pl.ds(far, WIDE)] = come[:, :WIDE]
    dq_out[:, pl.ds(own, WIDE)] = dq[...]
    dq_out[:, pl.ds(far, WIDE)] = come[:, WIDE:]


def join_kernel(info, here, sent, other, key_out, value_out):
    core = lax.rem(info[1], 2)
    mine = (here[...] + sent[...].astype(jnp.float32)).astype(jnp.bfloat16)
    own = pl.multiple_of(core * HD, HD)
    far = pl.multiple_of((1 - core) * HD, HD)
    key_out[:, pl.ds(own, HD)] = mine[:, :HD]
    key_out[:, pl.ds(far, HD)] = other[:, :HD]
    value_out[:, pl.ds(own, HD)] = mine[:, HD:]
    value_out[:, pl.ds(far, HD)] = other[:, HD:]


def call(kernel, name, width, info, operands):
    whole = pl.BlockSpec(memory_space=pltpu.VMEM)
    return pl.pallas_call(
        kernel,
        in_specs=[pl.BlockSpec(memory_space=pltpu.SMEM)] + [whole] * len(operands),
        out_specs=[whole] * 2,
        out_shape=[jax.ShapeDtypeStruct((ROWS, width), jnp.bfloat16)] * 2,
        compiler_params=pltpu.CompilerParams(vmem_limit_bytes=16 * 1024 * 1024),
        name=name,
    )(info, *operands)


def add(*terms):
    return sum(term.astype(jnp.float32) for term in terms).astype(jnp.bfloat16)


def body(queries, key_heads, value_heads, out_grad, lengths):
    count = lax.axis_size("stretch")
    stretch = lax.axis_index("stretch")
    h = lax.axis_index("head")
    core = lax.rem(stretch, 2)
    swap = [(s, s ^ 1) for s in range(count)]
    later = [(s, s + 2) for s in range(count - 2)]
    earlier = [(s + 2, s) for s in range(count - 2)]
    above, below = [
        [
            (s * RING + i, s * RING + (i + (1 if (s + i + turn) % 2 == 0 else -1)) % RING)
            for s in range(count)
            for i in range(RING)
        ]
        for turn in range(2)
    ]

    middle = 2 * ROWS

    def exchange(array, pairs):
        return lax.ppermute(array, ("stretch", "head"), pairs)

    def gather(held, neighbour):
        near = jnp.concatenate([held, neighbour], axis=0)
        second = exchange(near, below)
        third = exchange(second, above)
        return [near, second, third, exchange(third, below)]

    def scatter(here, near, second, third, fourth):
        third = add(third, exchange(fourth, below))
        second = add(second, exchange(third, above))
        come = exchange(second, below)
        return here + come[:middle].astype(jnp.float32), add(near, come[middle:])

    def half(array, which, width):
        return lax.dynamic_slice_in_dim(array, which * width, width, axis=1)

    def pair(which):
        return jnp.concatenate([half(key_heads, which, HD), half(value_heads, which, HD)], axis=1)

    own = jnp.concatenate([pair(core), lax.ppermute(pair(1 - core), "stretch", swap)], axis=0)
    leaving = [half(array, 1 - core, WIDE) for array in (queries, out_grad)]
    come = lax.ppermute(jnp.concatenate(leaving, axis=1), "stretch", swap)
    past = lax.ppermute(own, "stretch", later)
    slant = [(a, b + 2 * RING) for a, b in above if b + 2 * RING < count * RING]
    slanted = exchange(own, slant)
    info = jnp.stack([h, stretch]).astype(jnp.int32)
    operands = [queries, out_grad, come, *gather(own, exchange(own, above)), *gather(past, slanted)]
    outs = attend(info, lengths, operands)
    past_here, past_near = scatter(*outs[8:13])
    here, near = scatter(*outs[3:8])
    past_sum = past_here + exchange(past_near, above).astype(jnp.float32)
    sent_back = lax.ppermute(past_sum.astype(jnp.bfloat16), "stretch", earlier)
    near, swapped = lax.optimization_barrier((near, outs[2]))
    here = here + exchange(near, above).astype(jnp.float32)
    swapped = lax.ppermute(swapped, "stretch", swap)
    long = call(place_kernel, "place", 2 * WIDE, info, [outs[0], outs[1], swapped])
    attended, query_grad, here = lax.optimization_barrier((*long, here))
    other = lax.ppermute(add(here[ROWS:], sent_back[ROWS:]), "stretch", swap)
    short = call(join_kernel, "join", 2 * HD, info, [here[:ROWS], sent_back[:ROWS], other])
    return attended, query_grad, *short


def solution(mesh):
    spec = P(("dp", "stretch", "head"), None)
    return jax.shard_map(
        body,
        mesh=mesh,
        in_specs=(spec, spec, spec, spec, P("dp")),
        out_specs=(spec,) * 4,
        check_vma=False,
    )
```
